512 devices in a mesh: ctx: 64 (over x, y, core), head: 8 (over z).
Axes of the slice: x: 4, y: 8, z: 8, core: 2. Of those that a mesh axis runs over, the one named last changes fastest.
Arguments:
- queries: bfloat16 [32768, 5120], P('ctx', 'head'), may hold values from -6 to 6
- keys: bfloat16 [32768, 1024], P('ctx', 'head'), may hold values from -6 to 6
- values: bfloat16 [32768, 1024], P('ctx', 'head'), may hold values from -6 to 6
- kept: int32 [64, 32], P('ctx'), may hold values from 0 to 511
Outputs:
- attended: bfloat16 [32768, 5120], P(('ctx', 'head'))
The draws below stay inside these ranges and needn't reach their ends.
All inputs are finite; a program needn't handle non-finite values.
Results may differ from the reference program's by a relative error of at most 0.0033.
Values may be sent and summed in bfloat16 or wider, within the bound.
No kernel may reach another device: no remote copies, remote signals or barrier semaphores. Data moves between devices by JAX's collectives and lax.ppermute only.
A program may use at most 64 MiB of HBM per device.

```python
import math
import jax
import jax.numpy as jnp
from jax import lax

HQ = 40
KVH = 8
HD = 128
TOK_DEV = 512
ANCHOR = 128
PASS = 32
GROUP = 5
TOKENS = 32768
N_CTX = 64


def draw_queries(key, part):
    key = jax.random.fold_in(key, 1)
    return jnp.clip(1.5 * jax.random.normal(key, (TOKENS, HQ * HD), jnp.float32), -6.0, 6.0).astype(jnp.bfloat16)


def draw_keys(key, part):
    key = jax.random.fold_in(key, 2)
    return jnp.clip(1.5 * jax.random.normal(key, (TOKENS, KVH * HD), jnp.float32), -6.0, 6.0).astype(jnp.bfloat16)


def plant(values, stream_key, smallest, high):
    place = [jax.random.randint(jax.random.fold_in(stream_key, axis), (), 0, length) for axis, length in enumerate(values.shape)]
    widest = values.shape.index(max(values.shape))
    beside = place[:widest] + [(place[widest] + 1) % values.shape[widest]] + place[widest + 1:]
    return values.at[tuple(place)].set(smallest).at[tuple(beside)].set(high)


def block_levels(rng, dims, cuts, smallest, high):
    def one(position, parts):
        heights = jax.random.uniform(jax.random.fold_in(jax.random.fold_in(rng, 6), position), (parts,), jnp.float32, smallest / len(cuts), high / len(cuts))
        return jnp.repeat(jnp.exp(heights), dims[position] // parts).reshape((-1,) + (1,) * (len(dims) - position - 1))

    loudness = one(*cuts[0])
    for cut in cuts[1:]:
        loudness = loudness * one(*cut)
    return loudness


def normal_values(own_key, shape, deviation, most, shards=(), held_as=jnp.bfloat16):
    entries = jax.random.normal(own_key, shape, jnp.float32) * deviation
    if len(shards) > 0:
        entries = block_levels(own_key, shape, shards, -0.22, 0.18) * entries
    return jnp.clip(entries, min=-most, max=most).astype(held_as)


def setup_inputs(seed: int = 0) -> dict:
    seeds = jax.random.split(jax.random.key(seed), 5)
    return {
        "queries": draw_queries(jax.random.fold_in(seeds[4], 71), 0),
        "keys": draw_keys(jax.random.fold_in(seeds[4], 71), 0),
        "values": normal_values(seeds[2], (TOKENS, KVH * HD), 1.0, 6.0, ((0, 64), (1, 8))),
        "kept": plant(jax.random.randint(seeds[3], (N_CTX, PASS), 0, TOK_DEV), jax.random.fold_in(seeds[3], 1), 0, TOK_DEV - 1).astype(jnp.int32),
    }


def reference(queries, keys, values, kept):
    scale = 1.0 / math.sqrt(HD)
    block_keys = keys.reshape(N_CTX, TOK_DEV, KVH, HD)
    block_values = values.reshape(N_CTX, TOK_DEV, KVH, HD)
    index_table = kept[:, :, None, None].astype(jnp.int32)
    passing_keys = jnp.take_along_axis(block_keys, index_table, axis=1).reshape(N_CTX * PASS, KVH, HD)
    passing_values = jnp.take_along_axis(block_values, index_table, axis=1).reshape(N_CTX * PASS, KVH, HD)
    anchor_keys = keys[:ANCHOR].reshape(ANCHOR, KVH, HD)
    anchor_values = values[:ANCHOR].reshape(ANCHOR, KVH, HD)
    block_queries = queries.reshape(N_CTX, TOK_DEV, KVH, GROUP, HD)
    positions = jnp.arange(TOK_DEV, dtype=jnp.int32)
    causal = positions[None, :] <= positions[:, None]
    owners = jnp.arange(N_CTX * PASS, dtype=jnp.int32) // PASS

    def one_block(inputs):
        host_queries, host_keys, host_values, host_index = inputs
        all_keys = jnp.concatenate([anchor_keys, passing_keys, host_keys], 0)
        all_values = jnp.concatenate([anchor_values, passing_values, host_values], 0)
        anchor_ok = jnp.broadcast_to(host_index > 0, (TOK_DEV, ANCHOR))
        passing_ok = jnp.broadcast_to((owners < host_index)[None, :], (TOK_DEV, N_CTX * PASS))
        key_mask = jnp.concatenate([anchor_ok, passing_ok, causal], 1)
        scores = jnp.einsum('tkgd,skd->kgts', host_queries.astype(jnp.float32), all_keys.astype(jnp.float32)) * scale
        masked = jnp.where(key_mask, scores, -1e+30)
        largest = lax.optimization_barrier(jnp.max(masked, axis=-1, keepdims=True))
        weights = jnp.where(key_mask, jnp.exp(masked - largest), 0.0)
        totals = lax.optimization_barrier(jnp.sum(weights, axis=-1, keepdims=True))
        rounded = lax.optimization_barrier(weights.astype(jnp.bfloat16)).astype(jnp.float32)
        mixed = jnp.einsum('kgts,skd->tkgd', rounded, all_values.astype(jnp.float32))
        result = mixed / jnp.transpose(totals, (2, 0, 1, 3))
        return result.reshape(TOK_DEV, HQ * HD).astype(jnp.bfloat16)
    outputs = lax.map(one_block, (block_queries, block_keys, block_values, jnp.arange(N_CTX, dtype=jnp.int32)))
    return outputs.reshape(TOKENS, HQ * HD)
```

```python
import functools
import math

import jax
import jax.numpy as jnp
from jax import lax
from jax.experimental import pallas as pl
from jax.experimental.pallas import tpu as pltpu
from jax.sharding import PartitionSpec as P

HD = 128
ANCHOR = 128
PASS = 32
NX, NY, NC = 4, 8, 2
CHIPS = NX * NY
HALF = CHIPS * PASS
FAR = ANCHOR + 2 * HALF
ROWS = 512
TILE = 256
STEP = 16
NEG = -1e30
SCALE = math.log2(math.e) / math.sqrt(HD)


def ctx_of(x, y, core):
    return (x * NY + y) * NC + core


GROUPS_XY = [[ctx_of(x, y, c) for x in range(NX) for y in range(NY)] for c in range(NC)]
PAIRS_X = [[(0, ctx_of(x, 0, 0))] for x in range(1, NX)]
PAIRS_FAR = [(ctx_of(x, 0, 0), ctx_of(x, NY // 2, 0)) for x in range(NX)]
PAIRS_NEAR = [
    [(ctx_of(x, y, 0), ctx_of(x, y + step, 0)) for x in range(NX) for y in (0, NY // 2)]
    for step in range(1, NY // 2)
]
PAIRS_UP = [(ctx_of(x, y, 0), ctx_of(x, y, 1)) for x in range(NX) for y in range(NY)]
PAIRS_CORE = [(i, i ^ 1) for i in range(NX * NY * NC)]


def pick_kernel(kept_ref, key_ref, value_ref, sent_ref, start_ref):
    row = lax.broadcasted_iota(jnp.int32, (ROWS, PASS), 0)
    chosen = jnp.where(row == kept_ref[...], 1.0, 0.0).astype(jnp.bfloat16)
    for ref, base in ((key_ref, 0), (value_ref, PASS)):
        picked = lax.dot_general(
            chosen, ref[...], (((0,), (0,)), ((), ())), preferred_element_type=jnp.float32
        ).astype(jnp.bfloat16)
        for chip in range(CHIPS):
            sent_ref[chip, base : base + PASS, :] = picked
    first = lax.axis_index("ctx") == 0
    for ref, base in ((key_ref, 0), (value_ref, ANCHOR)):
        rows = ref[:ANCHOR, :]
        start_ref[base : base + ANCHOR, :] = jnp.where(first, rows, jnp.zeros_like(rows))


def pick(kept, keys, values):
    return pl.pallas_call(
        pick_kernel,
        out_shape=[
            jax.ShapeDtypeStruct((CHIPS, 2 * PASS, HD), jnp.bfloat16),
            jax.ShapeDtypeStruct((2 * ANCHOR, HD), jnp.bfloat16),
        ],
    )(kept, keys, values)


def attention_kernel(
    heads, q_ref, mine_ref, other_ref, anchor_ref, relayed_ref, key_ref, value_ref, out_ref, kx, kt, vx, s0, s1, p0, p1
):
    me = lax.axis_index("ctx")
    core = lax.rem(me, NC)

    anchor = anchor_ref[...] + relayed_ref[...]
    kx[0:ANCHOR, :] = anchor[:ANCHOR]
    vx[0:ANCHOR, :HD] = anchor[ANCHOR:]
    for ref, base in ((mine_ref, ANCHOR), (other_ref, ANCHOR + HALF)):
        for chip in range(CHIPS):
            at = slice(base + chip * PASS, base + (chip + 1) * PASS)
            kx[at, :] = ref[chip, :PASS, :]
            vx[at, :HD] = ref[chip, PASS:, :]
    kx[FAR:, :] = key_ref[...]
    vx[FAR:, :HD] = value_ref[...]
    vx[:, HD:] = jnp.ones((FAR + ROWS, HD), jnp.bfloat16)

    for start in range(0, FAR + ROWS, HD):
        kt[:HD, start : start + HD] = kx[start : start + HD, :].T
    row = lax.broadcasted_iota(jnp.int32, (HD, HALF), 0)
    at = lax.broadcasted_iota(jnp.int32, (HD, HALF), 1)
    never = jnp.where(row == 0, NEG, 0.0)
    kt[HD:, 0:ANCHOR] = jnp.where(row[:, :ANCHOR] * 0 < me, 0.0, never[:, :ANCHOR]).astype(
        jnp.bfloat16
    )
    for owner_core, base in ((core, ANCHOR), (1 - core, ANCHOR + HALF)):
        owner = NC * (at >> 5) + owner_core
        kt[HD:, base : base + HALF] = jnp.where(owner < me, 0.0, never).astype(jnp.bfloat16)
    kt[HD:, FAR:] = jnp.zeros((HD, ROWS), jnp.bfloat16)

    lane = lax.broadcasted_iota(jnp.int32, (TILE, HD), 1)
    flag = jnp.where(lane == 0, 1.0, 0.0).astype(jnp.bfloat16)
    items = [(head, tile) for head in range(heads) for tile in range(ROWS // TILE)]
    scores, weights = (s0, s1), (p0, p1)

    def width(tile):
        return FAR + (tile + 1) * TILE

    def score_columns(index):
        head, tile = items[index]
        rows = q_ref[tile * TILE : (tile + 1) * TILE, head * HD : (head + 1) * HD]
        queries = jnp.concatenate([rows, flag], 1)
        target = scores[index % 2]
        total = width(tile)
        for start in range(0, total, TILE):
            stop = min(start + TILE, total)
            yield target, start, stop, queries

    def score(piece):
        target, start, stop, queries = piece
        target[:, start:stop] = jnp.dot(
            queries, kt[:, start:stop], preferred_element_type=jnp.float32
        )

    for piece in score_columns(0):
        score(piece)
    for index, (head, tile) in enumerate(items):
        coming = list(score_columns(index + 1)) if index + 1 < len(items) else []
        total = width(tile)
        full = total - TILE
        source, target = scores[index % 2], weights[index % 2]
        for step in range(TILE // STEP):
            if step < len(coming):
                score(coming[step])
            r0 = step * STEP
            s = source[r0 : r0 + STEP, :total]
            at = lax.broadcasted_iota(jnp.int32, (STEP, TILE), 1)
            to = lax.broadcasted_iota(jnp.int32, (STEP, TILE), 0) + r0
            s = jnp.concatenate([s[:, :full], jnp.where(at <= to, s[:, full:], NEG)], 1)
            largest = jnp.max(s, axis=1, keepdims=True)
            target[r0 : r0 + STEP, :total] = jnp.exp2((s - largest) * SCALE).astype(jnp.bfloat16)
        for piece in coming[TILE // STEP :]:
            score(piece)
        mixed = jnp.dot(target[:, :total], vx[:total, :], preferred_element_type=jnp.float32)
        out_ref[tile * TILE : (tile + 1) * TILE, head * HD : (head + 1) * HD] = (
            mixed[:, :HD] / mixed[:, HD:]
        ).astype(jnp.bfloat16)


def attention(queries, mine, other, anchor, relayed, keys, values):
    heads = queries.shape[1] // HD
    return pl.pallas_call(
        functools.partial(attention_kernel, heads),
        out_shape=jax.ShapeDtypeStruct((ROWS, heads * HD), jnp.bfloat16),
        scratch_shapes=[
            pltpu.VMEM((FAR + ROWS, HD), jnp.bfloat16),
            pltpu.VMEM((2 * HD, FAR + ROWS), jnp.bfloat16),
            pltpu.VMEM((FAR + ROWS, 2 * HD), jnp.bfloat16),
            pltpu.VMEM((TILE, FAR + ROWS), jnp.float32),
            pltpu.VMEM((TILE, FAR + ROWS), jnp.float32),
            pltpu.VMEM((TILE, FAR + ROWS), jnp.bfloat16),
            pltpu.VMEM((TILE, FAR + ROWS), jnp.bfloat16),
        ],
        compiler_params=pltpu.CompilerParams(vmem_limit_bytes=40 * 1024 * 1024),
    )(queries, mine, other, anchor, relayed, keys, values)


def body(queries, keys, values, kept):
    sent, anchor = pick(kept, keys, values)
    mine = lax.all_to_all(sent, "ctx", 0, 0, axis_index_groups=GROUPS_XY)
    anchor = sum([lax.ppermute(anchor, "ctx", pairs) for pairs in PAIRS_X], anchor)
    anchor = anchor + lax.ppermute(anchor, "ctx", PAIRS_FAR)
    anchor = sum([lax.ppermute(anchor, "ctx", pairs) for pairs in PAIRS_NEAR], anchor)
    relayed = lax.ppermute(anchor, "ctx", PAIRS_UP)
    mine, anchor, relayed = lax.optimization_barrier((mine, anchor, relayed))
    other = lax.ppermute(mine, "ctx", PAIRS_CORE)

    attended = attention(queries, mine, other, anchor, relayed, keys, values)
    return lax.all_to_all(attended, "head", split_axis=0, concat_axis=1, tiled=True)


def solution(mesh):
    return jax.shard_map(
        body,
        mesh=mesh,
        in_specs=(P("ctx", "head"), P("ctx", "head"), P("ctx", "head"), P("ctx", None)),
        out_specs=P(("ctx", "head"), None),
        check_vma=False,
    )
```

```python
import functools
import math

import jax
import jax.numpy as jnp
from jax import lax
from jax.experimental import pallas as pl
from jax.experimental.pallas import tpu as pltpu
from jax.sharding import PartitionSpec as P

HD = 128
ANCHOR = 128
PASS = 32
NX, NY, NC = 4, 8, 2
CHIPS = NX * NY
HALF = CHIPS * PASS
FAR = 2 * HALF
ROWS = 512
TILE = 256
STEP = 16
SUBLANES = 8
NEG = -1e30
SCALE = math.log2(math.e) / math.sqrt(HD)


def ctx_of(x, y, core):
    return (x * NY + y) * NC + core


GROUPS_XY = [[ctx_of(x, y, c) for x in range(NX) for y in range(NY)] for c in range(NC)]
PAIRS_UP = [(0, 1)]
PAIRS_X = [[(c, ctx_of(x, 0, c)) for c in range(NC)] for x in range(1, NX)]
PAIRS_Y = {
    step: [
        (ctx_of(x, y, c), ctx_of(x, y + step, c))
        for x in range(NX)
        for y in range(0, NY, 2 * step)
        for c in range(NC)
    ]
    for step in (4, 2, 1)
}
PAIRS_CORE = [(i, i ^ 1) for i in range(NX * NY * NC)]


def pick_kernel(kept_ref, key_ref, value_ref, sent_ref, start_ref):
    row = lax.broadcasted_iota(jnp.int32, (ROWS, PASS), 0)
    chosen = jnp.where(row == kept_ref[...], 1.0, 0.0).astype(jnp.bfloat16)
    for ref, base in ((key_ref, 0), (value_ref, PASS)):
        picked = lax.dot_general(
            chosen, ref[...], (((0,), (0,)), ((), ())), preferred_element_type=jnp.float32
        ).astype(jnp.bfloat16)
        for chip in range(CHIPS):
            sent_ref[chip, base : base + PASS, :] = picked
    first = lax.axis_index("ctx") == 0
    for ref, base in ((key_ref, 0), (value_ref, ANCHOR)):
        rows = ref[:ANCHOR, :]
        start_ref[base : base + ANCHOR, :] = jnp.where(first, rows, jnp.zeros_like(rows))


def pick(kept, keys, values):
    return pl.pallas_call(
        pick_kernel,
        out_shape=[
            jax.ShapeDtypeStruct((CHIPS, 2 * PASS, HD), jnp.bfloat16),
            jax.ShapeDtypeStruct((2 * ANCHOR, HD), jnp.bfloat16),
        ],
    )(kept, keys, values)


def attention_kernel(
    heads, q_ref, mine_ref, other_ref, key_ref, value_ref, out_ref, log_ref,
    kx, kt, mask, vx, s0, s1, p0, p1, m0, m1,
):
    me = lax.axis_index("ctx")
    core = lax.rem(me, NC)

    for ref, base in ((mine_ref, 0), (other_ref, HALF)):
        for chip in range(CHIPS):
            at = slice(base + chip * PASS, base + (chip + 1) * PASS)
            kx[at, :] = ref[chip, :PASS, :]
            vx[at, :HD] = ref[chip, PASS:, :]
    kx[FAR:, :] = key_ref[...]
    vx[FAR:, :HD] = value_ref[...]
    vx[:, HD:] = jnp.ones((FAR + ROWS, HD), jnp.bfloat16)

    for start in range(0, FAR + ROWS, HD):
        kt[:, start : start + HD] = kx[start : start + HD, :].T
    at = lax.broadcasted_iota(jnp.int32, (SUBLANES, HALF), 1)
    for owner_core, base in ((core, 0), (1 - core, HALF)):
        owner = NC * (at >> 5) + owner_core
        mask[:, base : base + HALF] = jnp.where(owner < me, 0.0, NEG)

    items = [(head, tile) for head in range(heads) for tile in range(ROWS // TILE)]
    scores, weights = (s0, s1), (p0, p1)

    causal = lax.broadcasted_iota(jnp.int32, (TILE, TILE), 1) <= lax.broadcasted_iota(
        jnp.int32, (TILE, TILE), 0
    )

    def width(tile):
        return FAR + (tile + 1) * TILE

    def pieces(index):
        cuts = [*range(0, FAR, TILE), *range(FAR, width(items[index][1]) + 1, TILE)]
        return [(index, start, stop) for start, stop in zip(cuts[:-1], cuts[1:])]

    def score(index, start, stop):
        head, tile = items[index]
        rows = q_ref[tile * TILE : (tile + 1) * TILE, head * HD : (head + 1) * HD]
        found = jnp.dot(rows, kt[:, start:stop], preferred_element_type=jnp.float32)
        if stop <= FAR:
            found = found.reshape(TILE // SUBLANES, SUBLANES, TILE) + mask[:, start:stop][None]
            found = found.reshape(TILE, TILE)
        if stop == width(tile):
            found = jnp.where(causal, found, NEG)
        scores[index % 2][:, start:stop] = found
        peak = found[:, :HD]
        for at in range(HD, stop - start, HD):
            peak = jnp.maximum(peak, found[:, at : at + HD])
        peaks = (m0, m1)[index % 2]
        peaks[...] = peak if start == 0 else jnp.maximum(peaks[...], peak)

    for piece in pieces(0):
        score(*piece)
    for index, (head, tile) in enumerate(items):
        coming = pieces(index + 1) if index + 1 < len(items) else []
        total = width(tile)
        source, target, peaks = scores[index % 2], weights[index % 2], (m0, m1)[index % 2]
        largest = jnp.max(peaks[...], axis=1, keepdims=True)
        peaks[...] = jnp.broadcast_to(largest, (TILE, HD))
        for step in range(TILE // STEP):
            if step < len(coming):
                score(*coming[step])
            r0 = step * STEP
            most = jnp.concatenate([peaks[r0 : r0 + STEP, :]] * (total // HD), 1)
            target[r0 : r0 + STEP, :total] = jnp.exp2(
                (source[r0 : r0 + STEP, :total] - most) * SCALE
            ).astype(jnp.bfloat16)
        mixed = jnp.dot(target[:, :total], vx[:total, :], preferred_element_type=jnp.float32)
        at = (slice(tile * TILE, (tile + 1) * TILE), slice(head * HD, (head + 1) * HD))
        out_ref[at] = mixed[:, :HD] / mixed[:, HD:]
        log_ref[at] = peaks[...] * SCALE + jnp.log2(mixed[:, HD:])


def attention(queries, mine, other, keys, values):
    heads = queries.shape[1] // HD
    return pl.pallas_call(
        functools.partial(attention_kernel, heads),
        out_shape=[jax.ShapeDtypeStruct((ROWS, heads * HD), jnp.float32)] * 2,
        scratch_shapes=[
            pltpu.VMEM((FAR + ROWS, HD), jnp.bfloat16),
            pltpu.VMEM((HD, FAR + ROWS), jnp.bfloat16),
            pltpu.VMEM((SUBLANES, FAR), jnp.float32),
            pltpu.VMEM((FAR + ROWS, 2 * HD), jnp.bfloat16),
            pltpu.VMEM((TILE, FAR + ROWS), jnp.float32),
            pltpu.VMEM((TILE, FAR + ROWS), jnp.float32),
            pltpu.VMEM((TILE, FAR + ROWS), jnp.bfloat16),
            pltpu.VMEM((TILE, FAR + ROWS), jnp.bfloat16),
            pltpu.VMEM((TILE, HD), jnp.float32),
            pltpu.VMEM((TILE, HD), jnp.float32),
        ],
        compiler_params=pltpu.CompilerParams(vmem_limit_bytes=40 * 1024 * 1024),
    )(queries, mine, other, keys, values)


def join_kernel(heads, q_ref, part_ref, log_ref, *refs):
    *anchor_refs, out_ref = refs
    anchor = functools.reduce(jnp.add, [ref[...] for ref in anchor_refs])
    seen = lax.axis_index("ctx") > 0
    keys = anchor[:ANCHOR]
    values = jnp.concatenate([anchor[ANCHOR:], jnp.ones((ANCHOR, HD), jnp.bfloat16)], 1)
    for head in range(heads):
        columns = slice(head * HD, (head + 1) * HD)
        scores = lax.dot_general(
            q_ref[:, columns], keys, (((1,), (1,)), ((), ())), preferred_element_type=jnp.float32
        )
        scores = jnp.where(seen, scores, NEG)
        largest = jnp.max(scores, axis=1, keepdims=True)
        weights = jnp.exp2((scores - largest) * SCALE).astype(jnp.bfloat16)
        mixed = jnp.dot(weights, values, preferred_element_type=jnp.float32)
        before = log_ref[:, columns]
        top = jnp.maximum(before, largest * SCALE)
        old, new = jnp.exp2(before - top), jnp.exp2(largest * SCALE - top)
        out_ref[:, columns] = (
            (part_ref[:, columns] * old + mixed[:, :HD] * new) / (old + mixed[:, HD:] * new)
        ).astype(jnp.bfloat16)


def join(queries, part, log, anchors):
    return pl.pallas_call(
        functools.partial(join_kernel, queries.shape[1] // HD),
        out_shape=jax.ShapeDtypeStruct(queries.shape, jnp.bfloat16),
        compiler_params=pltpu.CompilerParams(vmem_limit_bytes=40 * 1024 * 1024),
    )(queries, part, log, *anchors)


def body(queries, keys, values, kept):
    sent, anchor = pick(kept, keys, values)
    up = lax.ppermute(anchor, "ctx", PAIRS_UP)
    sent, up = lax.optimization_barrier((sent, up))
    mine = lax.all_to_all(sent, "ctx", 0, 0, axis_index_groups=GROUPS_XY)
    anchor = anchor + up
    anchor = sum([lax.ppermute(anchor, "ctx", pairs) for pairs in PAIRS_X], anchor)
    for step in (4, 2):
        anchor = anchor + lax.ppermute(anchor, "ctx", PAIRS_Y[step])
    mine, anchor = lax.optimization_barrier((mine, anchor))
    anchors = [anchor, lax.ppermute(anchor, "ctx", PAIRS_Y[1])]
    other = lax.ppermute(mine, "ctx", PAIRS_CORE)

    part, log = attention(queries, mine, other, keys, values)
    attended = join(queries, part, log, anchors)
    return lax.all_to_all(attended, "head", split_axis=0, concat_axis=1, tiled=True)


def solution(mesh):
    return jax.shard_map(
        body,
        mesh=mesh,
        in_specs=(P("ctx", "head"), P("ctx", "head"), P("ctx", "head"), P("ctx", None)),
        out_specs=P(("ctx", "head"), None),
        check_vma=False,
    )
```

```python
import functools
import math

import jax
import jax.numpy as jnp
from jax import lax
from jax.experimental import pallas as pl
from jax.experimental.pallas import tpu as pltpu
from jax.sharding import PartitionSpec as P

HD = 128
ANCHOR = 128
PASS = 32
NX, NY, NC = 4, 8, 2
CHIPS = NX * NY
HALF = CHIPS * PASS
FAR = 2 * HALF
ROWS = 512
TILE = 256
STEP = 16
NEG = -1e30
SCALE = math.log2(math.e) / math.sqrt(HD)


def ctx_of(x, y, core):
    return (x * NY + y) * NC + core


GROUPS_XY = [[ctx_of(x, y, c) for x in range(NX) for y in range(NY)] for c in range(NC)]
PAIRS_UP = [(0, 1)]
PAIRS_X = [[(c, ctx_of(x, 0, c)) for c in range(NC)] for x in range(1, NX)]
PAIRS_Y = [
    [(ctx_of(x, y, c), ctx_of(x, to, c)) for x in range(NX) for y, to in hops for c in range(NC)]
    for hops in ([(0, 6)], [(0, 2), (6, 4)], [(0, 1), (2, 3), (4, 5), (6, 7)])
]
PAIRS_CORE = [(i, i ^ 1) for i in range(NX * NY * NC)]


def pick_kernel(kept_ref, key_ref, value_ref, sent_ref, start_ref):
    row = lax.broadcasted_iota(jnp.int32, (ROWS, PASS), 0)
    chosen = jnp.where(row == kept_ref[...], 1.0, 0.0).astype(jnp.bfloat16)
    for ref, base in ((key_ref, 0), (value_ref, PASS)):
        picked = lax.dot_general(
            chosen, ref[...], (((0,), (0,)), ((), ())), preferred_element_type=jnp.float32
        ).astype(jnp.bfloat16)
        for chip in range(CHIPS):
            sent_ref[chip, base : base + PASS, :] = picked
    first = lax.axis_index("ctx") == 0
    for ref, base in ((key_ref, 0), (value_ref, ANCHOR)):
        rows = ref[:ANCHOR, :]
        start_ref[base : base + ANCHOR, :] = jnp.where(first, rows, jnp.zeros_like(rows))


def pick(kept, keys, values):
    return pl.pallas_call(
        pick_kernel,
        out_shape=[
            jax.ShapeDtypeStruct((CHIPS, 2 * PASS, HD), jnp.bfloat16),
            jax.ShapeDtypeStruct((2 * ANCHOR, HD), jnp.bfloat16),
        ],
    )(kept, keys, values)


def attention_kernel(
    heads, q_ref, mine_ref, other_ref, key_ref, value_ref, out_ref, log_ref,
    kx, kt, vx, s0, s1, p0, p1, m0, m1,
):
    me = lax.axis_index("ctx")
    core = lax.rem(me, NC)

    for ref, base in ((mine_ref, 0), (other_ref, HALF)):
        for chip in range(CHIPS):
            at = slice(base + chip * PASS, base + (chip + 1) * PASS)
            kx[at, :] = ref[chip, :PASS, :]
            vx[at, :HD] = ref[chip, PASS:, :]
    kx[FAR:, :] = key_ref[...]
    vx[FAR:, :HD] = value_ref[...]
    vx[:, HD:] = jnp.ones((FAR + ROWS, HD), jnp.bfloat16)

    for start in range(0, FAR + ROWS, HD):
        kt[:HD, start : start + HD] = kx[start : start + HD, :].T
    row = lax.broadcasted_iota(jnp.int32, (HD, HALF), 0)
    at = lax.broadcasted_iota(jnp.int32, (HD, HALF), 1)
    never = jnp.where(row == 0, NEG, 0.0)
    for owner_core, base in ((core, 0), (1 - core, HALF)):
        owner = NC * (at >> 5) + owner_core
        kt[HD:, base : base + HALF] = jnp.where(owner < me, 0.0, never).astype(jnp.bfloat16)
    kt[HD:, FAR:] = jnp.zeros((HD, ROWS), jnp.bfloat16)

    lane = lax.broadcasted_iota(jnp.int32, (TILE, HD), 1)
    flag = jnp.where(lane == 0, 1.0, 0.0).astype(jnp.bfloat16)
    items = [(head, tile) for head in range(heads) for tile in range(ROWS // TILE)]
    scores, weights = (s0, s1), (p0, p1)

    causal = lax.broadcasted_iota(jnp.int32, (TILE, TILE), 1) <= lax.broadcasted_iota(
        jnp.int32, (TILE, TILE), 0
    )

    def width(tile):
        return FAR + (tile + 1) * TILE

    def pieces(index):
        cuts = [*range(0, FAR, TILE), *range(FAR, width(items[index][1]) + 1, TILE)]
        return [(index, start, stop) for start, stop in zip(cuts[:-1], cuts[1:])]

    def score(index, start, stop):
        head, tile = items[index]
        rows = q_ref[tile * TILE : (tile + 1) * TILE, head * HD : (head + 1) * HD]
        queries = jnp.concatenate([rows, flag], 1)
        found = jnp.dot(queries, kt[:, start:stop], preferred_element_type=jnp.float32)
        if stop == width(tile):
            found = jnp.where(causal, found, NEG)
        scores[index % 2][:, start:stop] = found
        peak = found[:, :HD]
        for at in range(HD, stop - start, HD):
            peak = jnp.maximum(peak, found[:, at : at + HD])
        peaks = (m0, m1)[index % 2]
        peaks[...] = peak if start == 0 else jnp.maximum(peaks[...], peak)

    for piece in pieces(0):
        score(*piece)
    for index, (head, tile) in enumerate(items):
        coming = pieces(index + 1) if index + 1 < len(items) else []
        total = width(tile)
        source, target, peaks = scores[index % 2], weights[index % 2], (m0, m1)[index % 2]
        largest = jnp.max(peaks[...], axis=1, keepdims=True)
        peaks[...] = jnp.broadcast_to(largest, (TILE, HD))
        for step in range(TILE // STEP):
            if step < len(coming):
                score(*coming[step])
            r0 = step * STEP
            most = jnp.concatenate([peaks[r0 : r0 + STEP, :]] * (total // HD), 1)
            target[r0 : r0 + STEP, :total] = jnp.exp2(
                (source[r0 : r0 + STEP, :total] - most) * SCALE
            ).astype(jnp.bfloat16)
        mixed = jnp.dot(target[:, :total], vx[:total, :], preferred_element_type=jnp.float32)
        at = (slice(tile * TILE, (tile + 1) * TILE), slice(head * HD, (head + 1) * HD))
        out_ref[at] = mixed[:, :HD] / mixed[:, HD:]
        log_ref[at] = peaks[...] * SCALE + jnp.log2(mixed[:, HD:])


def attention(queries, mine, other, keys, values):
    heads = queries.shape[1] // HD
    return pl.pallas_call(
        functools.partial(attention_kernel, heads),
        out_shape=[jax.ShapeDtypeStruct((ROWS, heads * HD), jnp.float32)] * 2,
        scratch_shapes=[
            pltpu.VMEM((FAR + ROWS, HD), jnp.bfloat16),
            pltpu.VMEM((2 * HD, FAR + ROWS), jnp.bfloat16),
            pltpu.VMEM((FAR + ROWS, 2 * HD), jnp.bfloat16),
            pltpu.VMEM((TILE, FAR + ROWS), jnp.float32),
            pltpu.VMEM((TILE, FAR + ROWS), jnp.float32),
            pltpu.VMEM((TILE, FAR + ROWS), jnp.bfloat16),
            pltpu.VMEM((TILE, FAR + ROWS), jnp.bfloat16),
            pltpu.VMEM((TILE, HD), jnp.float32),
            pltpu.VMEM((TILE, HD), jnp.float32),
        ],
        compiler_params=pltpu.CompilerParams(vmem_limit_bytes=40 * 1024 * 1024),
    )(queries, mine, other, keys, values)


def join_kernel(heads, q_ref, part_ref, log_ref, *refs):
    *anchor_refs, out_ref = refs
    anchor = functools.reduce(jnp.add, [ref[...] for ref in anchor_refs])
    seen = lax.axis_index("ctx") > 0
    keys = anchor[:ANCHOR]
    values = jnp.concatenate([anchor[ANCHOR:], jnp.ones((ANCHOR, HD), jnp.bfloat16)], 1)
    for head in range(heads):
        columns = slice(head * HD, (head + 1) * HD)
        scores = lax.dot_general(
            q_ref[:, columns], keys, (((1,), (1,)), ((), ())), preferred_element_type=jnp.float32
        )
        scores = jnp.where(seen, scores, NEG)
        largest = jnp.max(scores, axis=1, keepdims=True)
        weights = jnp.exp2((scores - largest) * SCALE).astype(jnp.bfloat16)
        mixed = jnp.dot(weights, values, preferred_element_type=jnp.float32)
        before = log_ref[:, columns]
        top = jnp.maximum(before, largest * SCALE)
        old, new = jnp.exp2(before - top), jnp.exp2(largest * SCALE - top)
        out_ref[:, columns] = (
            (part_ref[:, columns] * old + mixed[:, :HD] * new) / (old + mixed[:, HD:] * new)
        ).astype(jnp.bfloat16)


def join(queries, part, log, anchors):
    return pl.pallas_call(
        functools.partial(join_kernel, queries.shape[1] // HD),
        out_shape=jax.ShapeDtypeStruct(queries.shape, jnp.bfloat16),
        compiler_params=pltpu.CompilerParams(vmem_limit_bytes=40 * 1024 * 1024),
    )(queries, part, log, *anchors)


def body(queries, keys, values, kept):
    sent, anchor = pick(kept, keys, values)
    up = lax.ppermute(anchor, "ctx", PAIRS_UP)
    sent, up = lax.optimization_barrier((sent, up))
    mine = lax.all_to_all(sent, "ctx", 0, 0, axis_index_groups=GROUPS_XY)
    anchor = anchor + up
    anchor = sum([lax.ppermute(anchor, "ctx", pairs) for pairs in PAIRS_X], anchor)
    for pairs in PAIRS_Y[:2]:
        anchor = anchor + lax.ppermute(anchor, "ctx", pairs)
    mine, anchor = lax.optimization_barrier((mine, anchor))
    anchors = [anchor, lax.ppermute(anchor, "ctx", PAIRS_Y[2])]
    other = lax.ppermute(mine, "ctx", PAIRS_CORE)

    part, log = attention(queries, mine, other, keys, values)
    attended = join(queries, part, log, anchors)
    return lax.all_to_all(attended, "head", split_axis=0, concat_axis=1, tiled=True)


def solution(mesh):
    return jax.shard_map(
        body,
        mesh=mesh,
        in_specs=(P("ctx", "head"), P("ctx", "head"), P("ctx", "head"), P("ctx", None)),
        out_specs=P(("ctx", "head"), None),
        check_vma=False,
    )
```

```python
import functools
import math

import jax
import jax.numpy as jnp
from jax import lax
from jax.experimental import pallas as pl
from jax.experimental.pallas import tpu as pltpu
from jax.sharding import PartitionSpec as P

HD = 128
ANCHOR = 128
PASS = 32
NX, NY, NC = 4, 8, 2
CHIPS = NX * NY
HALF = CHIPS * PASS
FAR = 2 * HALF
ROWS = 512
TILE = 512
SPAN = 256
STEP = 16
PACE = 3
NEG = -1e30
SCALE = math.log2(math.e) / math.sqrt(HD)


def ctx_of(x, y, core):
    return (x * NY + y) * NC + core


GROUPS_XY = [[ctx_of(x, y, c) for x in range(NX) for y in range(NY)] for c in range(NC)]
PAIRS_UP = [(0, 1)]
PAIRS_X = [[(c, ctx_of(x, 0, c)) for c in range(NC)] for x in range(1, NX)]
PAIRS_Y = [
    [(ctx_of(x, y, c), ctx_of(x, to, c)) for x in range(NX) for y, to in hops for c in range(NC)]
    for hops in ([(0, 6)], [(0, 2), (6, 4)], [(0, 1), (2, 3), (4, 5), (6, 7)])
]
PAIRS_CORE = [(i, i ^ 1) for i in range(NX * NY * NC)]


def pick_kernel(kept_ref, key_ref, value_ref, sent_ref, start_ref):
    row = lax.broadcasted_iota(jnp.int32, (ROWS, PASS), 0)
    chosen = jnp.where(row == kept_ref[...], 1.0, 0.0).astype(jnp.bfloat16)
    for ref, base in ((key_ref, 0), (value_ref, PASS)):
        picked = lax.dot_general(
            chosen, ref[...], (((0,), (0,)), ((), ())), preferred_element_type=jnp.float32
        ).astype(jnp.bfloat16)
        for chip in range(CHIPS):
            sent_ref[chip, base : base + PASS, :] = picked
    first = lax.axis_index("ctx") == 0
    for ref, base in ((key_ref, 0), (value_ref, ANCHOR)):
        rows = ref[:ANCHOR, :]
        start_ref[base : base + ANCHOR, :] = jnp.where(first, rows, jnp.zeros_like(rows))


def pick(kept, keys, values):
    return pl.pallas_call(
        pick_kernel,
        out_shape=[
            jax.ShapeDtypeStruct((CHIPS, 2 * PASS, HD), jnp.bfloat16),
            jax.ShapeDtypeStruct((2 * ANCHOR, HD), jnp.bfloat16),
        ],
    )(kept, keys, values)


def attention_kernel(
    heads, q_ref, mine_ref, other_ref, key_ref, value_ref, out_ref, log_ref,
    kx, kt, vx, s0, s1, p0, p1, m0, m1,
):
    me = lax.axis_index("ctx")
    core = lax.rem(me, NC)

    for ref, base in ((mine_ref, 0), (other_ref, HALF)):
        for chip in range(CHIPS):
            at = slice(base + chip * PASS, base + (chip + 1) * PASS)
            kx[at, :] = ref[chip, :PASS, :]
            vx[at, :HD] = ref[chip, PASS:, :]
    kx[FAR:, :] = key_ref[...]
    vx[FAR:, :HD] = value_ref[...]
    vx[:, HD:] = jnp.ones((FAR + ROWS, HD), jnp.bfloat16)

    for start in range(0, FAR + ROWS, HD):
        kt[:HD, start : start + HD] = kx[start : start + HD, :].T
    row = lax.broadcasted_iota(jnp.int32, (HD, HALF), 0)
    at = lax.broadcasted_iota(jnp.int32, (HD, HALF), 1)
    never = jnp.where(row == 0, NEG, 0.0)
    for owner_core, base in ((core, 0), (1 - core, HALF)):
        owner = NC * (at >> 5) + owner_core
        kt[HD:, base : base + HALF] = jnp.where(owner < me, 0.0, never).astype(jnp.bfloat16)
    kt[HD:, FAR:] = jnp.zeros((HD, ROWS), jnp.bfloat16)

    lane = lax.broadcasted_iota(jnp.int32, (TILE, HD), 1)
    flag = jnp.where(lane == 0, 1.0, 0.0).astype(jnp.bfloat16)
    items = [(head, tile) for head in range(heads) for tile in range(ROWS // TILE)]
    scores, weights = (s0, s1), (p0, p1)

    ahead = lax.broadcasted_iota(jnp.int32, (TILE, SPAN), 1) - lax.broadcasted_iota(
        jnp.int32, (TILE, SPAN), 0
    )

    def width(tile):
        return FAR + (tile + 1) * TILE

    def pieces(index):
        cuts = range(0, width(items[index][1]) + 1, SPAN)
        return [(index, start, stop) for start, stop in zip(cuts[:-1], cuts[1:])]

    def score(index, start, stop):
        head, tile = items[index]
        rows = q_ref[tile * TILE : (tile + 1) * TILE, head * HD : (head + 1) * HD]
        queries = jnp.concatenate([rows, flag], 1)
        found = jnp.dot(queries, kt[:, start:stop], preferred_element_type=jnp.float32)
        if stop > FAR + tile * TILE:
            found = jnp.where(ahead <= FAR + tile * TILE - start, found, NEG)
        scores[index % 2][:, start:stop] = found
        peak = found[:, :HD]
        for at in range(HD, stop - start, HD):
            peak = jnp.maximum(peak, found[:, at : at + HD])
        peaks = (m0, m1)[index % 2]
        peaks[...] = peak if start == 0 else jnp.maximum(peaks[...], peak)

    for piece in pieces(0):
        score(*piece)
    for index, (head, tile) in enumerate(items):
        coming = pieces(index + 1) if index + 1 < len(items) else []
        total = width(tile)
        source, target, peaks = scores[index % 2], weights[index % 2], (m0, m1)[index % 2]
        largest = jnp.max(peaks[...], axis=1, keepdims=True)
        peaks[...] = jnp.broadcast_to(largest, (TILE, HD))
        for step in range(TILE // STEP):
            if step % PACE == 0 and step // PACE < len(coming):
                score(*coming[step // PACE])
            r0 = step * STEP
            most = jnp.concatenate([peaks[r0 : r0 + STEP, :]] * (total // HD), 1)
            target[r0 : r0 + STEP, :total] = jnp.exp2(
                (source[r0 : r0 + STEP, :total] - most) * SCALE
            ).astype(jnp.bfloat16)
        mixed = jnp.dot(target[:, :total], vx[:total, :], preferred_element_type=jnp.float32)
        at = (slice(tile * TILE, (tile + 1) * TILE), slice(head * HD, (head + 1) * HD))
        out_ref[at] = mixed[:, :HD] / mixed[:, HD:]
        log_ref[at] = peaks[...] * SCALE + jnp.log2(mixed[:, HD:])


def attention(queries, mine, other, keys, values):
    heads = queries.shape[1] // HD
    return pl.pallas_call(
        functools.partial(attention_kernel, heads),
        out_shape=[jax.ShapeDtypeStruct((ROWS, heads * HD), jnp.float32)] * 2,
        scratch_shapes=[
            pltpu.VMEM((FAR + ROWS, HD), jnp.bfloat16),
            pltpu.VMEM((2 * HD, FAR + ROWS), jnp.bfloat16),
            pltpu.VMEM((FAR + ROWS, 2 * HD), jnp.bfloat16),
            pltpu.VMEM((TILE, FAR + ROWS), jnp.float32),
            pltpu.VMEM((TILE, FAR + ROWS), jnp.float32),
            pltpu.VMEM((TILE, FAR + ROWS), jnp.bfloat16),
            pltpu.VMEM((TILE, FAR + ROWS), jnp.bfloat16),
            pltpu.VMEM((TILE, HD), jnp.float32),
            pltpu.VMEM((TILE, HD), jnp.float32),
        ],
        compiler_params=pltpu.CompilerParams(vmem_limit_bytes=40 * 1024 * 1024),
    )(queries, mine, other, keys, values)


def join_kernel(heads, q_ref, part_ref, log_ref, *refs):
    *anchor_refs, out_ref = refs
    anchor = functools.reduce(jnp.add, [ref[...] for ref in anchor_refs])
    seen = lax.axis_index("ctx") > 0
    keys = anchor[:ANCHOR]
    values = jnp.concatenate([anchor[ANCHOR:], jnp.ones((ANCHOR, HD), jnp.bfloat16)], 1)
    for head in range(heads):
        columns = slice(head * HD, (head + 1) * HD)
        scores = lax.dot_general(
            q_ref[:, columns], keys, (((1,), (1,)), ((), ())), preferred_element_type=jnp.float32
        )
        scores = jnp.where(seen, scores, NEG)
        largest = jnp.max(scores, axis=1, keepdims=True)
        weights = jnp.exp2((scores - largest) * SCALE).astype(jnp.bfloat16)
        mixed = jnp.dot(weights, values, preferred_element_type=jnp.float32)
        before = log_ref[:, columns]
        top = jnp.maximum(before, largest * SCALE)
        old, new = jnp.exp2(before - top), jnp.exp2(largest * SCALE - top)
        out_ref[:, columns] = (
            (part_ref[:, columns] * old + mixed[:, :HD] * new) / (old + mixed[:, HD:] * new)
        ).astype(jnp.bfloat16)


def join(queries, part, log, anchors):
    return pl.pallas_call(
        functools.partial(join_kernel, queries.shape[1] // HD),
        out_shape=jax.ShapeDtypeStruct(queries.shape, jnp.bfloat16),
        compiler_params=pltpu.CompilerParams(vmem_limit_bytes=40 * 1024 * 1024),
    )(queries, part, log, *anchors)


def body(queries, keys, values, kept):
    sent, anchor = pick(kept, keys, values)
    up = lax.ppermute(anchor, "ctx", PAIRS_UP)
    sent, up = lax.optimization_barrier((sent, up))
    mine = lax.all_to_all(sent, "ctx", 0, 0, axis_index_groups=GROUPS_XY)
    anchor = anchor + up
    anchor = sum([lax.ppermute(anchor, "ctx", pairs) for pairs in PAIRS_X], anchor)
    for pairs in PAIRS_Y[:2]:
        anchor = anchor + lax.ppermute(anchor, "ctx", pairs)
    mine, anchor = lax.optimization_barrier((mine, anchor))
    anchors = [anchor, lax.ppermute(anchor, "ctx", PAIRS_Y[2])]
    other = lax.ppermute(mine, "ctx", PAIRS_CORE)

    part, log = attention(queries, mine, other, keys, values)
    attended = join(queries, part, log, anchors)
    return lax.all_to_all(attended, "head", split_axis=0, concat_axis=1, tiled=True)


def solution(mesh):
    return jax.shard_map(
        body,
        mesh=mesh,
        in_specs=(P("ctx", "head"), P("ctx", "head"), P("ctx", "head"), P("ctx", None)),
        out_specs=P(("ctx", "head"), None),
        check_vma=False,
    )
```

```python
import functools
import math

import jax
import jax.numpy as jnp
from jax import lax
from jax.experimental import pallas as pl
from jax.experimental.pallas import tpu as pltpu
from jax.sharding import PartitionSpec as P

HD = 128
ANCHOR = 128
PASS = 32
NX, NY, NC = 4, 8, 2
CHIPS = NX * NY
HALF = CHIPS * PASS
FAR = 2 * HALF
ROWS = 512
TILE = 256
STEP = 16
NEG = -1e30
SCALE = math.log2(math.e) / math.sqrt(HD)


def ctx_of(x, y, core):
    return (x * NY + y) * NC + core


GROUPS_XY = [[ctx_of(x, y, c) for x in range(NX) for y in range(NY)] for c in range(NC)]
PAIRS_UP = [(0, 1)]
PAIRS_X = [[(c, ctx_of(x, 0, c)) for c in range(NC)] for x in (3, 2, 1)]
PAIRS_Y = [
    [(ctx_of(x, y, c), ctx_of(x, to, c)) for x in range(NX) for y, to in hops for c in range(NC)]
    for hops in ([(0, 6)], [(0, 2), (6, 4)], [(0, 1), (2, 3), (4, 5), (6, 7)])
]
PAIRS_CORE = [(i, i ^ 1) for i in range(NX * NY * NC)]


def pick_kernel(kept_ref, key_ref, value_ref, sent_ref, start_ref):
    row = lax.broadcasted_iota(jnp.int32, (ROWS, PASS), 0)
    chosen = jnp.where(row == kept_ref[...], 1.0, 0.0).astype(jnp.bfloat16)
    for ref, base in ((key_ref, 0), (value_ref, PASS)):
        picked = lax.dot_general(
            chosen, ref[...], (((0,), (0,)), ((), ())), preferred_element_type=jnp.float32
        ).astype(jnp.bfloat16)
        for chip in range(CHIPS):
            sent_ref[chip, base : base + PASS, :] = picked
    first = lax.axis_index("ctx") == 0
    for ref, base in ((key_ref, 0), (value_ref, ANCHOR)):
        rows = ref[:ANCHOR, :]
        start_ref[base : base + ANCHOR, :] = jnp.where(first, rows, jnp.zeros_like(rows))


def pick(kept, keys, values):
    return pl.pallas_call(
        pick_kernel,
        out_shape=[
            jax.ShapeDtypeStruct((CHIPS, 2 * PASS, HD), jnp.bfloat16),
            jax.ShapeDtypeStruct((2 * ANCHOR, HD), jnp.bfloat16),
        ],
    )(kept, keys, values)


def attention_kernel(heads, *refs):
    for x in range(NX):
        pl.when(lax.axis_index("ctx") // (NY * NC) == x)(
            functools.partial(attend, heads, (x + 1) * NY, *refs)
        )


def attend(
    heads, chips, q_ref, mine_ref, other_ref, key_ref, value_ref, out_ref, log_ref,
    kx, kt, vx, s0, s1, p0, p1, m0, m1,
):
    me = lax.axis_index("ctx")
    core = lax.rem(me, NC)
    half = chips * PASS
    far = 2 * half

    for ref, base in ((mine_ref, 0), (other_ref, half)):
        for chip in range(chips):
            at = slice(base + chip * PASS, base + (chip + 1) * PASS)
            kx[at, :] = ref[chip, :PASS, :]
            vx[at, :HD] = ref[chip, PASS:, :]
    kx[far : far + ROWS, :] = key_ref[...]
    vx[far : far + ROWS, :HD] = value_ref[...]
    vx[: far + ROWS, HD:] = jnp.ones((far + ROWS, HD), jnp.bfloat16)

    for start in range(0, far + ROWS, HD):
        kt[:HD, start : start + HD] = kx[start : start + HD, :].T
    row = lax.broadcasted_iota(jnp.int32, (HD, half), 0)
    at = lax.broadcasted_iota(jnp.int32, (HD, half), 1)
    never = jnp.where(row == 0, NEG, 0.0)
    for owner_core, base in ((core, 0), (1 - core, half)):
        owner = NC * (at >> 5) + owner_core
        kt[HD:, base : base + half] = jnp.where(owner < me, 0.0, never).astype(jnp.bfloat16)
    kt[HD:, far : far + ROWS] = jnp.zeros((HD, ROWS), jnp.bfloat16)

    lane = lax.broadcasted_iota(jnp.int32, (TILE, HD), 1)
    flag = jnp.where(lane == 0, 1.0, 0.0).astype(jnp.bfloat16)
    items = [(head, tile) for head in range(heads) for tile in range(ROWS // TILE)]
    scores, weights = (s0, s1), (p0, p1)

    causal = lax.broadcasted_iota(jnp.int32, (TILE, TILE), 1) <= lax.broadcasted_iota(
        jnp.int32, (TILE, TILE), 0
    )

    def width(tile):
        return far + (tile + 1) * TILE

    def pieces(index):
        cuts = [*range(0, far, TILE), *range(far, width(items[index][1]) + 1, TILE)]
        return [(index, start, stop) for start, stop in zip(cuts[:-1], cuts[1:])]

    def score(index, start, stop):
        head, tile = items[index]
        rows = q_ref[tile * TILE : (tile + 1) * TILE, head * HD : (head + 1) * HD]
        queries = jnp.concatenate([rows, flag], 1)
        found = jnp.dot(queries, kt[:, start:stop], preferred_element_type=jnp.float32)
        if stop == width(tile):
            found = jnp.where(causal, found, NEG)
        scores[index % 2][:, start:stop] = found
        peak = found[:, :HD]
        for at in range(HD, stop - start, HD):
            peak = jnp.maximum(peak, found[:, at : at + HD])
        peaks = (m0, m1)[index % 2]
        peaks[...] = peak if start == 0 else jnp.maximum(peaks[...], peak)

    for piece in pieces(0):
        score(*piece)
    for index, (head, tile) in enumerate(items):
        coming = pieces(index + 1) if index + 1 < len(items) else []
        total = width(tile)
        source, target, peaks = scores[index % 2], weights[index % 2], (m0, m1)[index % 2]
        largest = jnp.max(peaks[...], axis=1, keepdims=True)
        peaks[...] = jnp.broadcast_to(largest, (TILE, HD))
        for step in range(TILE // STEP):
            if step < len(coming):
                score(*coming[step])
            r0 = step * STEP
            most = jnp.concatenate([peaks[r0 : r0 + STEP, :]] * (total // HD), 1)
            target[r0 : r0 + STEP, :total] = jnp.exp2(
                (source[r0 : r0 + STEP, :total] - most) * SCALE
            ).astype(jnp.bfloat16)
        mixed = jnp.dot(target[:, :total], vx[:total, :], preferred_element_type=jnp.float32)
        at = (slice(tile * TILE, (tile + 1) * TILE), slice(head * HD, (head + 1) * HD))
        out_ref[at] = mixed[:, :HD] / mixed[:, HD:]
        log_ref[at] = peaks[...] * SCALE + jnp.log2(mixed[:, HD:])


def attention(queries, mine, other, keys, values):
    heads = queries.shape[1] // HD
    return pl.pallas_call(
        functools.partial(attention_kernel, heads),
        out_shape=[jax.ShapeDtypeStruct((ROWS, heads * HD), jnp.float32)] * 2,
        scratch_shapes=[
            pltpu.VMEM((FAR + ROWS, HD), jnp.bfloat16),
            pltpu.VMEM((2 * HD, FAR + ROWS), jnp.bfloat16),
            pltpu.VMEM((FAR + ROWS, 2 * HD), jnp.bfloat16),
            pltpu.VMEM((TILE, FAR + ROWS), jnp.float32),
            pltpu.VMEM((TILE, FAR + ROWS), jnp.float32),
            pltpu.VMEM((TILE, FAR + ROWS), jnp.bfloat16),
            pltpu.VMEM((TILE, FAR + ROWS), jnp.bfloat16),
            pltpu.VMEM((TILE, HD), jnp.float32),
            pltpu.VMEM((TILE, HD), jnp.float32),
        ],
        compiler_params=pltpu.CompilerParams(vmem_limit_bytes=40 * 1024 * 1024),
    )(queries, mine, other, keys, values)


def join_kernel(heads, q_ref, part_ref, log_ref, *refs):
    *anchor_refs, out_ref = refs
    anchor = functools.reduce(jnp.add, [ref[...] for ref in anchor_refs])
    seen = lax.axis_index("ctx") > 0
    keys = anchor[:ANCHOR]
    values = jnp.concatenate([anchor[ANCHOR:], jnp.ones((ANCHOR, HD), jnp.bfloat16)], 1)
    for head in range(heads):
        columns = slice(head * HD, (head + 1) * HD)
        scores = lax.dot_general(
            q_ref[:, columns], keys, (((1,), (1,)), ((), ())), preferred_element_type=jnp.float32
        )
        scores = jnp.where(seen, scores, NEG)
        largest = jnp.max(scores, axis=1, keepdims=True)
        weights = jnp.exp2((scores - largest) * SCALE).astype(jnp.bfloat16)
        mixed = jnp.dot(weights, values, preferred_element_type=jnp.float32)
        before = log_ref[:, columns]
        top = jnp.maximum(before, largest * SCALE)
        old, new = jnp.exp2(before - top), jnp.exp2(largest * SCALE - top)
        out_ref[:, columns] = (
            (part_ref[:, columns] * old + mixed[:, :HD] * new) / (old + mixed[:, HD:] * new)
        ).astype(jnp.bfloat16)


def join(queries, part, log, anchors):
    return pl.pallas_call(
        functools.partial(join_kernel, queries.shape[1] // HD),
        out_shape=jax.ShapeDtypeStruct(queries.shape, jnp.bfloat16),
        compiler_params=pltpu.CompilerParams(vmem_limit_bytes=40 * 1024 * 1024),
    )(queries, part, log, *anchors)


def body(queries, keys, values, kept):
    sent, anchor = pick(kept, keys, values)
    up = lax.ppermute(anchor, "ctx", PAIRS_UP)
    sent, up = lax.optimization_barrier((sent, up))
    mine = lax.all_to_all(sent, "ctx", 0, 0, axis_index_groups=GROUPS_XY)
    anchor = anchor + up
    anchor = sum([lax.ppermute(anchor, "ctx", pairs) for pairs in PAIRS_X], anchor)
    for pairs in PAIRS_Y[:2]:
        anchor = anchor + lax.ppermute(anchor, "ctx", pairs)
    mine, anchor = lax.optimization_barrier((mine, anchor))
    anchors = [anchor, lax.ppermute(anchor, "ctx", PAIRS_Y[2])]
    other = lax.ppermute(mine, "ctx", PAIRS_CORE)

    part, log = attention(queries, mine, other, keys, values)
    attended = join(queries, part, log, anchors)
    return lax.all_to_all(attended, "head", split_axis=0, concat_axis=1, tiled=True)


def solution(mesh):
    return jax.shard_map(
        body,
        mesh=mesh,
        in_specs=(P("ctx", "head"), P("ctx", "head"), P("ctx", "head"), P("ctx", None)),
        out_specs=P(("ctx", "head"), None),
        check_vma=False,
    )
```
